256 devices in a mesh: dp: 2 (over core), depth: 8 (over y, z_lo), row: 4 (over x), col: 4 (over z_hi).
Axes of the slice: x: 4, y: 4, z: 8 (z_hi: 4, z_lo: 2; z = z_hi * 2 + z_lo), core: 2. Of those that a mesh axis runs over, the one named last changes fastest.
Arguments:
- grad_out: bfloat16 [16384, 6144], P(('dp', 'depth', 'row'), 'col'), may hold values from -12 to 12
- queries: bfloat16 [16384, 6144], P(('dp', 'depth', 'col'), 'row'), may hold values from -12 to 12
- keys: bfloat16 [16384, 6144], P(('dp', 'depth', 'col'), 'row'), may hold values from -12 to 12
- values: bfloat16 [16384, 6144], P(('dp', 'depth', 'col'), 'row'), may hold values from -6 to 6
- out_weight: bfloat16 [48, 128, 6144], P('row', ('dp', 'depth'), 'col'), may hold values from -0.078125 to 0.078125
Outputs:
- grad_queries: bfloat16 [16384, 6144], P(('dp', 'depth', 'col'), 'row')
- grad_keys: bfloat16 [16384, 6144], P(('dp', 'depth', 'col'), 'row')
- grad_values: bfloat16 [16384, 6144], P(('dp', 'depth', 'col'), 'row')
- grad_weight: float32 [48, 128, 6144], P('row', ('dp', 'depth'), 'col')
The draws below stay inside these ranges and needn't reach their ends.
All inputs are finite; a program needn't handle non-finite values.
Results may differ from the reference program's by a relative error of at most 0.023.
Values may be sent and summed in bfloat16 or wider, within the bound.
No kernel may reach another device: no remote copies, remote signals or barrier semaphores. Data moves between devices by JAX's collectives and lax.ppermute only.
A program may use at most 128 MiB of HBM per device.

```python
import math
import jax
import jax.numpy as jnp
from jax import lax

D = 6144
HEADS = 48
HEAD_DIM = 128
PATCHES = 256
TOKENS = 16384


def rough_rows(seed_key):
    scale_key, base_key = jax.random.split(seed_key)
    row_scales = jnp.exp(jax.random.uniform(scale_key, (TOKENS, 1), jnp.float32, math.log(0.4), math.log(4.0)))
    base = jnp.clip(jax.random.normal(base_key, (TOKENS, D), jnp.float32), -3.0, 3.0)
    return base * row_scales


def draw_queries(key, part):
    seed_key = jax.random.fold_in(key, 11)
    result = rough_rows(seed_key)
    return result.astype(jnp.bfloat16)


def draw_keys(key, part):
    seed_key = jax.random.fold_in(key, 23)
    result = rough_rows(seed_key)
    return result.astype(jnp.bfloat16)


def level_of(key, shape, cuts, least, largest):
    gain, own = 1.0, jax.random.fold_in(key, 6)
    for axis_at, parts in cuts:
        heights = jnp.exp(jax.random.uniform(jax.random.fold_in(own, axis_at), (parts,), jnp.float32, least / len(cuts), largest / len(cuts)))
        gain = gain * jnp.repeat(heights, shape[axis_at] // parts).reshape([-1 if axis == axis_at else 1 for axis in range(len(shape))])
    return gain


def scatter_about(key, shape, deviation, limit, cuts=(), held_as=jnp.bfloat16):
    array = deviation * jax.random.normal(key, shape, jnp.float32)
    if cuts:
        array = array * level_of(key, shape, cuts, -0.22, 0.18)
    return jnp.clip(array, -limit, limit).astype(held_as)


def setup_inputs(seed: int = 0) -> dict:
    seeds = jax.random.split(jax.random.key(seed), 6)
    grad_out = scatter_about(seeds[0], (TOKENS, D), 2.0, 12.0, ((0, 64), (1, 4)))
    queries = draw_queries(jax.random.fold_in(seeds[5], 71), 0)
    keys = draw_keys(jax.random.fold_in(seeds[5], 71), 0)
    values = scatter_about(seeds[3], (TOKENS, D), 1.0, 6.0, ((0, 64), (1, 4)))
    out_weight = scatter_about(seeds[4], (HEADS, HEAD_DIM, D), D ** -0.5, 0.078125, ((0, 4), (1, 16), (2, 4)))
    return dict(grad_out=grad_out, queries=queries, keys=keys, values=values, out_weight=out_weight)


def softmax_rows(scores):
    highest = jnp.max(scores, axis=-1, keepdims=True)
    weights = jnp.exp(scores - highest)
    return weights / jnp.sum(weights, axis=-1, keepdims=True)


def image_terms(query_img, key_img, value_img, grad_img, flat_weight):
    scale = HEAD_DIM ** -0.5
    shaped = (PATCHES, HEADS, HEAD_DIM)
    grad_ctx = jnp.dot(grad_img, flat_weight.T, preferred_element_type=jnp.float32).astype(jnp.bfloat16)
    query_heads = query_img.reshape(shaped).astype(jnp.float32)
    key_heads = key_img.reshape(shaped).astype(jnp.float32)
    value_heads = value_img.reshape(shaped).astype(jnp.float32)
    grad_heads = grad_ctx.reshape(shaped).astype(jnp.float32)
    scores = jnp.einsum("qhd,khd->hqk", query_heads, key_heads) * scale
    probs = softmax_rows(scores)
    probs_low = lax.optimization_barrier(probs.astype(jnp.bfloat16)).astype(jnp.float32)
    context = jnp.einsum("hqk,khd->qhd", probs_low, value_heads).astype(jnp.bfloat16).reshape(PATCHES, D)
    grad_probs = jnp.einsum("qhd,khd->hqk", grad_heads, value_heads)
    inner = jnp.sum(probs * grad_probs, axis=-1, keepdims=True)
    grad_scores = (probs * (grad_probs - inner) * scale).astype(jnp.bfloat16)
    grad_scores = lax.optimization_barrier(grad_scores).astype(jnp.float32)
    grad_query = jnp.einsum("hqk,khd->qhd", grad_scores, key_heads).astype(jnp.bfloat16).reshape(PATCHES, D)
    grad_key = jnp.einsum("hqk,qhd->khd", grad_scores, query_heads).astype(jnp.bfloat16).reshape(PATCHES, D)
    grad_value = jnp.einsum("hqk,qhd->khd", probs_low, grad_heads).astype(jnp.bfloat16).reshape(PATCHES, D)
    weight_term = jnp.dot(context.T, grad_img, preferred_element_type=jnp.float32)
    return grad_query, grad_key, grad_value, weight_term


def reference(grad_out, queries, keys, values, out_weight):
    flat_weight = out_weight.reshape(D, D)
    images = TOKENS // PATCHES

    def visit(running, packed):
        query_img, key_img, value_img, grad_img = packed
        grad_query, grad_key, grad_value, weight_term = image_terms(query_img, key_img, value_img, grad_img, flat_weight)
        return running + weight_term, (grad_query, grad_key, grad_value)

    stacked = tuple(source.reshape(images, PATCHES, D) for source in (queries, keys, values, grad_out))
    running, outputs = lax.scan(visit, jnp.zeros((D, D), jnp.float32), stacked)
    grad_weight = (running * (TOKENS ** -0.5)).reshape(HEADS, HEAD_DIM, D)
    return (outputs[0].reshape(TOKENS, D), outputs[1].reshape(TOKENS, D), outputs[2].reshape(TOKENS, D), grad_weight)
```

```python
import functools

import jax
import jax.numpy as jnp
from jax import lax
from jax.experimental import pallas as pl
from jax.experimental.pallas import tpu as pltpu
from jax.sharding import PartitionSpec as P

HEAD_DIM = 128
PATCHES = 256
SCALE = HEAD_DIM ** (-0.5)
EXP2_SCALE = SCALE * 1.4426950408889634
LAYER = 4
HEADS_PER_STEP = 4


def dot(a, b, dims):
    return lax.dot_general(a, b, (dims, ((), ())), preferred_element_type=jnp.float32)


def probs_kq(q, k):
    scores = dot(k, q, ((1,), (1,)))
    highest = jnp.max(scores, axis=0, keepdims=True)
    weights = jnp.exp2((scores - highest) * EXP2_SCALE)
    return weights * (1.0 / jnp.sum(weights, axis=0, keepdims=True))


def forward_kernel(q_ref, k_ref, v_ref, ctx_ref):
    for h in range(HEADS_PER_STEP):
        cols = slice(h * HEAD_DIM, (h + 1) * HEAD_DIM)
        probs = probs_kq(q_ref[:, cols], k_ref[:, cols]).astype(jnp.bfloat16)
        ctx_ref[cols, :] = dot(v_ref[:, cols], probs, ((0,), (0,))).astype(jnp.bfloat16)


def backward_kernel(q_ref, k_ref, v_ref, g_ref, gq_ref, gk_ref, gv_ref):
    for h in range(HEADS_PER_STEP):
        cols = slice(h * HEAD_DIM, (h + 1) * HEAD_DIM)
        q, k, v, g = q_ref[:, cols], k_ref[:, cols], v_ref[:, cols], g_ref[:, cols]
        probs = probs_kq(q, k)
        gv_ref[:, cols] = dot(probs.astype(jnp.bfloat16), g, ((1,), (0,))).astype(jnp.bfloat16)
        grad_probs = dot(v, g, ((1,), (1,)))
        inner = jnp.sum(probs * grad_probs, axis=0, keepdims=True)
        grad_scores = (probs * (grad_probs - inner) * SCALE).astype(jnp.bfloat16)
        gk_ref[:, cols] = dot(grad_scores, q, ((1,), (0,))).astype(jnp.bfloat16)
        gq_ref[:, cols] = dot(grad_scores, k, ((0,), (0,))).astype(jnp.bfloat16)


def attention_forward(q, k, v):
    tokens, feats = q.shape
    wide = HEADS_PER_STEP * HEAD_DIM
    block = pl.BlockSpec((tokens, wide), lambda i: (0, i))
    return pl.pallas_call(
        forward_kernel,
        grid=(feats // wide,),
        in_specs=[block] * 3,
        out_specs=pl.BlockSpec((wide, tokens), lambda i: (i, 0)),
        out_shape=jax.ShapeDtypeStruct((feats, tokens), jnp.bfloat16),
        cost_estimate=pl.CostEstimate(
            flops=4 * tokens * tokens * feats, bytes_accessed=8 * tokens * feats, transcendentals=0
        ),
    )(q, k, v)


def attention_backward(q, k, v, g):
    tokens, feats = q.shape
    wide = HEADS_PER_STEP * HEAD_DIM
    block = pl.BlockSpec((tokens, wide), lambda i: (0, i))
    return pl.pallas_call(
        backward_kernel,
        grid=(feats // wide,),
        in_specs=[block] * 4,
        out_specs=[block] * 3,
        out_shape=[jax.ShapeDtypeStruct((tokens, feats), jnp.bfloat16)] * 3,
        cost_estimate=pl.CostEstimate(
            flops=10 * tokens * tokens * feats, bytes_accessed=14 * tokens * feats, transcendentals=0
        ),
    )(q, k, v, g)


def ring(step, size=4):
    return [(i, (i + step) % size) for i in range(size)]


def depth_ring(step):
    return [(2 * y + low, 2 * ((y + step) % 4) + low) for y in range(4) for low in range(2)]


def gather_ring(block, axis):
    half = block.shape[0] // 2
    up, down = ring(1), ring(-1)
    a, b = block[:half], block[half:]
    below_a = lax.ppermute(a, axis, up)
    above_b = lax.ppermute(b, axis, down)
    below_b = lax.ppermute(b, axis, up)
    above_a = lax.ppermute(a, axis, down)
    across_a = lax.ppermute(below_a, axis, up)
    across_b = lax.ppermute(above_b, axis, down)
    return [(a, b), (above_a, above_b), (across_a, across_b), (below_a, below_b)]


def add(a, b):
    return a.astype(jnp.float32) + b.astype(jnp.float32)


def scatter_ring(parts, axis, up, down, split):
    low = jnp.bfloat16
    (a0, b0), (a1, b1), (a2, b2), (a3, b3) = [split(p) for p in parts]
    from_a = lax.ppermute(a2, axis, up)
    from_b = lax.ppermute(b2, axis, down)
    up_b = lax.ppermute(b1, axis, up)
    down_a = lax.ppermute(a3, axis, down)
    up_a = lax.ppermute(add(a1, from_a).astype(low), axis, up)
    down_b = lax.ppermute(add(b3, from_b).astype(low), axis, down)
    return add(a0, down_a) + up_a.astype(jnp.float32), add(b0, up_b) + down_b.astype(jnp.float32)


def shards(grad_out, queries, keys, values, out_weight):
    row_count, feat_width = queries.shape
    head_count = out_weight.shape[0]
    out_width = grad_out.shape[1]
    low = jnp.bfloat16
    row, col = lax.axis_index("row"), lax.axis_index("col")
    dp, depth = lax.axis_index("dp"), lax.axis_index("depth")

    full_weight = lax.all_gather(out_weight, ("dp", "depth"), axis=1, tiled=True).reshape(
        feat_width, out_width
    )
    context = attention_forward(queries, keys, values)
    gathered = gather_ring(grad_out, "row")
    layer_grad = jnp.zeros((LAYER, 2, row_count // 2, out_width), low)
    for offset, halves in enumerate(gathered):
        slot = lax.rem(row + offset - col + LAYER, LAYER)
        layer_grad = lax.dynamic_update_slice(layer_grad, jnp.stack(halves)[None], (slot, 0, 0, 0))
    layer_grad = layer_grad.reshape(LAYER, row_count, out_width)
    contexts = gather_ring(context, "col")
    contexts = [jnp.concatenate(halves, axis=0) for halves in contexts]

    partial_ctx = [dot(layer_grad[k], full_weight, ((1,), (1,))).astype(low) for k in range(LAYER)]
    wide = feat_width // 2
    grad_a, grad_b = scatter_ring(
        partial_ctx, "col", ring(1), ring(-1), lambda p: (p[:, :wide], p[:, wide:])
    )
    grad_ctx = jnp.concatenate([grad_a.astype(low), grad_b.astype(low)], axis=1)
    grad_query, grad_key, grad_value = attention_backward(queries, keys, values, grad_ctx)

    layer_ctx = jnp.concatenate(contexts, axis=1)
    partial_weight = dot(layer_ctx, layer_grad.reshape(LAYER * row_count, out_width), ((1,), (0,)))
    shaped = partial_weight.reshape(head_count, 2, 4, 2, HEAD_DIM // 16, out_width)
    mine = lax.dynamic_index_in_dim(shaped, dp, 1, keepdims=False)
    other = lax.dynamic_index_in_dim(shaped, 1 - dp, 1, keepdims=False).astype(low)
    paired = add(mine, lax.ppermute(other, "dp", [(0, 1), (1, 0)]))
    paired = paired.astype(low)
    y, z_low = depth // 2, lax.rem(depth, 2)
    quarters = [
        lax.dynamic_index_in_dim(paired, lax.rem(y + k, 4), 1, keepdims=False) for k in range(4)
    ]
    half = head_count // 2
    sums = scatter_ring(
        quarters, "depth", depth_ring(1), depth_ring(-1), lambda p: (p[:half], p[half:])
    )
    summed = jnp.concatenate(sums, axis=0)
    mine = lax.dynamic_index_in_dim(summed, z_low, 1, keepdims=False)
    other = lax.dynamic_index_in_dim(summed, 1 - z_low, 1, keepdims=False).astype(low)
    grad_weight = add(mine, lax.ppermute(other, "depth", [(i, i ^ 1) for i in range(8)]))
    all_tokens = row_count * lax.axis_size("col") * lax.axis_size("dp") * lax.axis_size("depth")
    grad_weight = grad_weight * all_tokens ** (-0.5)
    return grad_query, grad_key, grad_value, grad_weight


def solution(mesh):
    in_specs = (
        P(("dp", "depth", "row"), "col"),
        P(("dp", "depth", "col"), "row"),
        P(("dp", "depth", "col"), "row"),
        P(("dp", "depth", "col"), "row"),
        P("row", ("dp", "depth"), "col"),
    )
    out_specs = (
        P(("dp", "depth", "col"), "row"),
        P(("dp", "depth", "col"), "row"),
        P(("dp", "depth", "col"), "row"),
        P("row", ("dp", "depth"), "col"),
    )
    return jax.shard_map(shards, mesh=mesh, in_specs=in_specs, out_specs=out_specs, check_vma=False)
```

```python
import functools

import jax
import jax.numpy as jnp
from jax import lax
from jax.experimental import pallas as pl
from jax.experimental.pallas import tpu as pltpu
from jax.sharding import PartitionSpec as P

HEAD_DIM = 128
PATCHES = 256
SCALE = HEAD_DIM ** (-0.5)
EXP2_SCALE = SCALE * 1.4426950408889634
LAYER = 4
GROUPS = 2
LOW = jnp.bfloat16
SLOTS = ((0, 1, 2, 3), (0, 3, 1, 2))


def dot(a, b, dims):
    return lax.dot_general(a, b, (dims, ((), ())), preferred_element_type=jnp.float32)


def add(a, b):
    return a.astype(jnp.float32) + b.astype(jnp.float32)


def after(value, *earlier):
    return lax.optimization_barrier((value, earlier))[0]


def forward_kernel(q_ref, k_ref, v_ref, ctx_a, ctx_b, norm_ref):
    early = pl.program_id(0) < pl.num_programs(0) // 2
    contexts = []
    for h in range(norm_ref.shape[0]):
        cols = slice(h * HEAD_DIM, (h + 1) * HEAD_DIM)
        scores = dot(k_ref[:, cols], q_ref[:, cols], ((1,), (1,)))
        highest = jnp.max(scores, axis=0, keepdims=True)
        weights = jnp.exp2((scores - highest) * EXP2_SCALE)
        total = jnp.sum(weights, axis=0, keepdims=True)
        probs = (weights * (1.0 / total)).astype(LOW)
        contexts.append(dot(v_ref[:, cols], probs, ((0,), (0,))).astype(LOW))
        norm_ref[h] = highest * EXP2_SCALE + jnp.log2(total)
    for ctx_ref, here in ((ctx_a, early), (ctx_b, jnp.logical_not(early))):

        @pl.when(here)
        def _(ctx_ref=ctx_ref):
            for h, context in enumerate(contexts):
                ctx_ref[h * HEAD_DIM : (h + 1) * HEAD_DIM, :] = context


def attention_forward(q, k, v):
    tokens, feats = q.shape
    group = 3
    wide = group * HEAD_DIM
    block = pl.BlockSpec((tokens, wide), lambda i: (0, i))
    return pl.pallas_call(
        forward_kernel,
        grid=(feats // wide,),
        in_specs=[block] * 3,
        out_specs=[
            pl.BlockSpec((wide, tokens), lambda i: (jnp.minimum(i, 1), 0)),
            pl.BlockSpec((wide, tokens), lambda i: (jnp.maximum(i - 2, 0), 0)),
            pl.BlockSpec((group, 1, tokens), lambda i: (i, 0, 0)),
        ],
        out_shape=[
            jax.ShapeDtypeStruct((feats // 2, tokens), LOW),
            jax.ShapeDtypeStruct((feats // 2, tokens), LOW),
            jax.ShapeDtypeStruct((feats // HEAD_DIM, 1, tokens), jnp.float32),
        ],
        cost_estimate=pl.CostEstimate(
            flops=4 * tokens * tokens * feats, bytes_accessed=8 * tokens * feats, transcendentals=0
        ),
    )(q, k, v)


def backward_kernel(q_ref, k_ref, v_ref, norm_ref, *rest):
    firsts, seconds = rest[:3], rest[3:6]
    gq_ref, gk_ref, gv_ref = rest[-3:]
    heads = norm_ref.shape[0]
    for h in range(heads):
        cols = slice(h * HEAD_DIM, (h + 1) * HEAD_DIM)
        q, k, v = q_ref[:, cols], k_ref[:, cols], v_ref[:, cols]
        terms, at = (firsts, h) if h < heads // 2 else (seconds, h - heads // 2)
        a, b, c = [ref[:, at * HEAD_DIM : (at + 1) * HEAD_DIM].astype(jnp.float32) for ref in terms]
        g = (a + b + c).astype(LOW)
        scores = dot(k, q, ((1,), (1,)))
        probs = jnp.exp2(scores * EXP2_SCALE - norm_ref[h])
        gv_ref[:, cols] = dot(probs.astype(LOW), g, ((1,), (0,))).astype(LOW)
        grad_probs = dot(v, g, ((1,), (1,)))
        inner = jnp.sum(probs * grad_probs, axis=0, keepdims=True)
        grad_scores = (probs * (grad_probs - inner) * SCALE).astype(LOW)
        gk_ref[:, cols] = dot(grad_scores, q, ((1,), (0,))).astype(LOW)
        gq_ref[:, cols] = dot(grad_scores, k, ((0,), (0,))).astype(LOW)


def attention_backward(group, q, k, v, norm, terms, last_terms, earlier):
    tokens, feats = q.shape
    wide = feats // GROUPS
    heads = wide // HEAD_DIM
    block = pl.BlockSpec((tokens, wide), lambda i: (0, group))
    half = pl.BlockSpec((tokens, wide // 2), lambda i: (0, group))
    last = pl.BlockSpec((tokens, wide // 2), lambda i: (0, 0))
    norms = pl.BlockSpec((heads, 1, tokens), lambda i: (group, 0, 0))
    sums = (*terms[0], last_terms[0], *terms[1], last_terms[1])
    return pl.pallas_call(
        backward_kernel,
        grid=(1,),
        in_specs=[block] * 3
        + [norms]
        + [half, half, last] * 2
        + [pl.BlockSpec(memory_space=pl.ANY)] * len(earlier),
        out_specs=[block] * 3,
        out_shape=[jax.ShapeDtypeStruct((tokens, feats), LOW)] * 3,
        input_output_aliases={4 + len(sums) + i: i for i in range(len(earlier))},
        compiler_params=pltpu.CompilerParams(vmem_limit_bytes=32 * 2**20),
        cost_estimate=pl.CostEstimate(
            flops=100 * tokens * tokens * wide, bytes_accessed=16 * tokens * wide, transcendentals=0
        ),
    )(q, k, v, norm, *sums, *earlier)


def context_grad_kernel(offsets, places, *rest):
    w_mine, w_other, a_ref, outs, w_all = rest[:4], rest[4:8], rest[8], rest[9:-1], rest[-1]
    x, y, z, dp = places[0], places[1], places[2], places[3]
    for k in range(4):
        slot = lax.rem(y + k, 4)
        for pieces, half in ((w_mine, dp), (w_other, 1 - dp)):
            rows = pl.ds(pl.multiple_of((half * 4 + slot) * 16, 16), 16)
            w_all[:, rows, :] = pieces[k][...]
    heads, size, width = w_all.shape
    weight = w_all[...].reshape(heads * size, width)
    middle = heads // 2 * size
    for i, k in enumerate(offsets):
        product = dot(a_ref[lax.rem(z + k - x + 4, 4)], weight, ((1,), (1,))).astype(LOW)
        outs[2 * i][...] = product[:, :middle]
        outs[2 * i + 1][...] = product[:, middle:]


def context_grad(offsets, places, w_mine, w_other, layer_grad):
    heads, width = w_mine[0].shape[0], w_mine[0].shape[2]
    group = heads // GROUPS
    half = group // 2 * HEAD_DIM
    piece = pl.BlockSpec((group, 16, width), lambda i, p: (i, 0, 0))
    count = 2 * len(offsets)
    return pl.pallas_call(
        functools.partial(context_grad_kernel, offsets),
        grid_spec=pltpu.PrefetchScalarGridSpec(
            num_scalar_prefetch=1,
            grid=(GROUPS,),
            in_specs=[piece] * 8 + [pl.BlockSpec(layer_grad.shape, lambda i, p: (0, 0, 0))],
            out_specs=[pl.BlockSpec((PATCHES, half), lambda i, p: (0, i))] * count,
            scratch_shapes=[pltpu.VMEM((group, HEAD_DIM, width), LOW)],
        ),
        out_shape=[jax.ShapeDtypeStruct((PATCHES, GROUPS * half), LOW)] * count,
        compiler_params=pltpu.CompilerParams(vmem_limit_bytes=32 * 2**20),
        cost_estimate=pl.CostEstimate(
            flops=2 * PATCHES * heads * HEAD_DIM, bytes_accessed=2**16, transcendentals=0
        ),
    )(places, *w_mine, *w_other, layer_grad)


def weight_grad_kernel(places, *rest):
    ctx_a, ctx_b, a_ref, rest = rest[:4], rest[4:8], rest[8], rest[9:]
    mine_refs, other_refs, total = rest[:4], rest[4:8], rest[8]
    x, y, z, dp = places[0], places[1], places[2], places[3]
    late = pl.program_id(0) >= pl.num_programs(0) // 2
    acc = None
    for k in range(LAYER):
        ctx = jnp.where(late, ctx_b[k][...], ctx_a[k][...])
        term = dot(ctx, a_ref[lax.rem(z + k - x + 4, 4)], ((1,), (0,)))
        acc = term if acc is None else acc + term
    total[...] = acc
    for h in range(mine_refs[0].shape[0]):
        for slot in range(4):
            part = lax.rem(y + jnp.where(late, SLOTS[1][slot], SLOTS[0][slot]), 4)
            for refs, half in ((mine_refs, dp), (other_refs, 1 - dp)):
                rows = pl.ds(pl.multiple_of(h * HEAD_DIM + (half * 4 + part) * 16, 16), 16)
                refs[slot][h] = total[rows, :].astype(LOW)


def weight_grad(places, contexts, layer_grad):
    feats, tokens = 2 * contexts[0][0].shape[0], contexts[0][0].shape[1]
    width = layer_grad.shape[2]
    heads, group = feats // HEAD_DIM, 2
    steps = heads // group
    ctx_a = pl.BlockSpec((group * HEAD_DIM, tokens), lambda i, p: (jnp.minimum(i, steps // 2 - 1), 0))
    ctx_b = pl.BlockSpec((group * HEAD_DIM, tokens), lambda i, p: (jnp.maximum(i - steps // 2, 0), 0))
    out = pl.BlockSpec((group, 16, width), lambda i, p: (i, 0, 0))
    return pl.pallas_call(
        weight_grad_kernel,
        grid_spec=pltpu.PrefetchScalarGridSpec(
            num_scalar_prefetch=1,
            grid=(steps,),
            in_specs=[ctx_a] * 4
            + [ctx_b] * 4
            + [pl.BlockSpec(layer_grad.shape, lambda i, p: (0, 0, 0))],
            out_specs=[out] * 8,
            scratch_shapes=[pltpu.VMEM((group * HEAD_DIM, width), jnp.float32)],
        ),
        out_shape=[jax.ShapeDtypeStruct((heads, 16, width), LOW)] * 8,
        compiler_params=pltpu.CompilerParams(vmem_limit_bytes=32 * 2**20),
        cost_estimate=pl.CostEstimate(
            flops=2 * PATCHES * feats, bytes_accessed=2**16, transcendentals=0
        ),
    )(places, *contexts[0], *contexts[1], layer_grad)


def shards(grad_out, queries, keys, values, out_weight):
    row_count, feat_width = queries.shape
    head_count = out_weight.shape[0]
    out_width = grad_out.shape[1]
    dp, depth = lax.axis_index("dp"), lax.axis_index("depth")
    y, z_low = depth // 2, lax.rem(depth, 2)
    places = jnp.stack([lax.axis_index("row"), y, lax.axis_index("col"), dp])
    rings = {
        name: [[(i, (i + step) % size) for i in range(size)] for step in steps]
        for name, size, steps in (("row", 4, (1, -1)), ("col", 4, (1, -1)), ("depth", 8, (2, -2)))
    }
    z_pair = [(i, i ^ 1) for i in range(8)]
    core_pair = [(0, 1), (1, 0)]

    def both(axis, for_up, for_down):
        up, down = rings[axis]
        return lax.ppermute(for_up, axis, up), lax.ppermute(for_down, axis, down)

    def gather_across(axis, below, above):
        half = below.shape[0] // 2
        return jnp.concatenate(both(axis, below[:half], above[half:]), axis=0)

    w_next = lax.ppermute(out_weight, "depth", z_pair)
    g_below, g_above = both("row", grad_out, grad_out)
    ctx_a, ctx_b, norm = attention_forward(queries, keys, values)
    c_below_a, c_above_b = both("col", ctx_a, ctx_b)

    w_next = after(w_next, ctx_a)
    first = jnp.where(z_low == 0, out_weight, w_next)
    second = jnp.where(z_low == 0, w_next, out_weight)
    w_own = jnp.stack([first, second], axis=1).reshape(head_count, 16, out_width)
    w_own, ctx_a, ctx_b, g_above, g_below, c_below_a, c_above_b = after(
        (w_own, ctx_a, ctx_b, g_above, g_below, c_below_a, c_above_b)
    )
    c_below_b, c_above_a = both("col", ctx_b, ctx_a)
    w_below, w_above = both("depth", w_own, w_own)
    g_across = lax.ppermute(g_below, "row", rings["row"][0])

    w_below, w_above, c_below_a, c_above_b, c_below_b, c_above_a, g_across = after(
        (w_below, w_above, c_below_a, c_above_b, c_below_b, c_above_a, g_across)
    )
    c_across_a, c_across_b = both("col", c_below_a, c_above_b)
    w_across = gather_across("depth", w_below, w_above)
    w_mine = [w_own, w_above, w_across, w_below]
    layer_grad = jnp.stack([grad_out, g_above, g_across, g_below])
    w_mine, c_across_a, c_across_b, layer_grad = after((w_mine, c_across_a, c_across_b, layer_grad))
    w_other = [lax.ppermute(piece, "dp", core_pair) for piece in w_mine]
    contexts = (ctx_a, c_above_a, c_across_a, c_below_a), (ctx_b, c_above_b, c_across_b, c_below_b)

    a2, b2 = context_grad((2,), places, w_mine, w_other, layer_grad)
    up_a, down_b = both("col", a2, b2)
    places = after(places, a2, b2)
    a0, b0, a1, b1, a3, b3 = context_grad((0, 1, 3), places, w_mine, w_other, layer_grad)
    b1, a3, up_a, down_b = after((b1, a3, up_a, down_b))
    up_b, down_a = both("col", b1, a3)
    contexts = after(contexts, a0)
    both_halves = weight_grad(places, contexts, layer_grad)
    both_halves = after(both_halves, up_a, down_b)
    paired = [
        add(mine, lax.ppermute(other, "dp", core_pair)).astype(LOW)
        for mine, other in zip(both_halves[:4], both_halves[4:])
    ]
    half = head_count // 2
    up, down = both("depth", paired[2], paired[3])
    up, down, up_b, down_a, up_a, down_b = after((up, down, up_b, down_a, up_a, down_b))
    wide = feat_width // GROUPS // 2
    lasts = []
    for g in range(GROUPS):
        cols = slice(g * wide, (g + 1) * wide)
        for_up = add(a1[:, cols], up_a[:, cols]).astype(LOW)
        for_down = add(b3[:, cols], down_b[:, cols]).astype(LOW)
        lasts.append(both("col", for_up, for_down))
    last_up, last_down = both(
        "depth",
        add(paired[1][:half], up[:half]).astype(LOW),
        add(paired[1][half:], down[half:]).astype(LOW),
    )
    summed = jnp.concatenate(
        [
            add(paired[0][:half], down[:half]) + last_up,
            add(paired[0][half:], up[half:]) + last_down,
        ],
        axis=0,
    ).reshape(head_count, 2, 8, out_width)
    mine = jnp.where(z_low == 0, summed[:, 0], summed[:, 1])
    other = jnp.where(z_low == 0, summed[:, 1], summed[:, 0]).astype(LOW)
    other = after(other, lasts[0])
    grad_weight = add(mine, lax.ppermute(other, "depth", z_pair))
    all_tokens = row_count * lax.axis_size("col") * lax.axis_size("dp") * lax.axis_size("depth")
    grad_weight = grad_weight * all_tokens ** (-0.5)

    grads = ()
    for g in range(GROUPS):
        terms = (a0, down_a), (b0, up_b)
        grads = attention_backward(g, queries, keys, values, norm, terms, lasts[g], grads)
    return (*grads, grad_weight)


def solution(mesh):
    in_specs = (
        P(("dp", "depth", "row"), "col"),
        P(("dp", "depth", "col"), "row"),
        P(("dp", "depth", "col"), "row"),
        P(("dp", "depth", "col"), "row"),
        P("row", ("dp", "depth"), "col"),
    )
    out_specs = (
        P(("dp", "depth", "col"), "row"),
        P(("dp", "depth", "col"), "row"),
        P(("dp", "depth", "col"), "row"),
        P("row", ("dp", "depth"), "col"),
    )
    return jax.shard_map(shards, mesh=mesh, in_specs=in_specs, out_specs=out_specs, check_vma=False)
```

```python
import functools

import jax
import jax.numpy as jnp
from jax import lax
from jax.experimental import pallas as pl
from jax.experimental.pallas import tpu as pltpu
from jax.sharding import PartitionSpec as P

HEAD_DIM = 128
PATCHES = 256
SCALE = HEAD_DIM ** (-0.5)
EXP2_SCALE = SCALE * 1.4426950408889634
LAYER = 4
GROUPS = 2
LOW = jnp.bfloat16
SLOTS = ((0, 1, 2, 3), (0, 3, 1, 2))


def dot(a, b, dims):
    return lax.dot_general(a, b, (dims, ((), ())), preferred_element_type=jnp.float32)


def add(a, b):
    return a.astype(jnp.float32) + b.astype(jnp.float32)


def after(value, *earlier):
    return lax.optimization_barrier((value, earlier))[0]


def forward_kernel(q_ref, k_ref, v_ref, ctx_ref, norm_ref):
    for h in range(norm_ref.shape[0]):
        cols = slice(h * HEAD_DIM, (h + 1) * HEAD_DIM)
        scores = dot(k_ref[:, cols], q_ref[:, cols], ((1,), (1,)))
        highest = jnp.max(scores, axis=0, keepdims=True)
        weights = jnp.exp2((scores - highest) * EXP2_SCALE)
        total = jnp.sum(weights, axis=0, keepdims=True)
        probs = (weights * (1.0 / total)).astype(LOW)
        ctx_ref[cols, :] = dot(v_ref[:, cols], probs, ((0,), (0,))).astype(LOW)
        norm_ref[h] = highest * EXP2_SCALE + jnp.log2(total)


def attention_forward(q, k, v):
    tokens, feats = q.shape
    group = 4
    wide = group * HEAD_DIM
    block = pl.BlockSpec((tokens, wide), lambda i: (0, i))
    return pl.pallas_call(
        forward_kernel,
        grid=(feats // wide,),
        in_specs=[block] * 3,
        out_specs=[
            pl.BlockSpec((wide, tokens), lambda i: (i, 0)),
            pl.BlockSpec((group, 1, tokens), lambda i: (i, 0, 0)),
        ],
        out_shape=[
            jax.ShapeDtypeStruct((feats, tokens), LOW),
            jax.ShapeDtypeStruct((feats // HEAD_DIM, 1, tokens), jnp.float32),
        ],
        cost_estimate=pl.CostEstimate(
            flops=4 * tokens * tokens * feats, bytes_accessed=8 * tokens * feats, transcendentals=0
        ),
    )(q, k, v)


def backward_kernel(q_ref, k_ref, v_ref, norm_ref, *rest):
    firsts, seconds = rest[:3], rest[3:6]
    gq_ref, gk_ref, gv_ref = rest[-3:]
    heads = norm_ref.shape[0]
    for h in range(heads):
        cols = slice(h * HEAD_DIM, (h + 1) * HEAD_DIM)
        q, k, v = q_ref[:, cols], k_ref[:, cols], v_ref[:, cols]
        terms, at = (firsts, h) if h < heads // 2 else (seconds, h - heads // 2)
        a, b, c = [ref[:, at * HEAD_DIM : (at + 1) * HEAD_DIM].astype(jnp.float32) for ref in terms]
        g = (a + b + c).astype(LOW)
        scores = dot(k, q, ((1,), (1,)))
        probs = jnp.exp2(scores * EXP2_SCALE - norm_ref[h])
        gv_ref[:, cols] = dot(probs.astype(LOW), g, ((1,), (0,))).astype(LOW)
        grad_probs = dot(v, g, ((1,), (1,)))
        inner = jnp.sum(probs * grad_probs, axis=0, keepdims=True)
        grad_scores = (probs * (grad_probs - inner) * SCALE).astype(LOW)
        gk_ref[:, cols] = dot(grad_scores, q, ((1,), (0,))).astype(LOW)
        gq_ref[:, cols] = dot(grad_scores, k, ((0,), (0,))).astype(LOW)


def attention_backward(group, q, k, v, norm, terms, last_terms, earlier):
    tokens, feats = q.shape
    wide = feats // GROUPS
    heads = wide // HEAD_DIM
    block = pl.BlockSpec((tokens, wide), lambda i: (0, group))
    half = pl.BlockSpec((tokens, wide // 2), lambda i: (0, group))
    last = pl.BlockSpec((tokens, wide // 2), lambda i: (0, 0))
    norms = pl.BlockSpec((heads, 1, tokens), lambda i: (group, 0, 0))
    sums = (*terms[0], last_terms[0], *terms[1], last_terms[1])
    return pl.pallas_call(
        backward_kernel,
        grid=(1,),
        in_specs=[block] * 3
        + [norms]
        + [half, half, last] * 2
        + [pl.BlockSpec(memory_space=pl.ANY)] * len(earlier),
        out_specs=[block] * 3,
        out_shape=[jax.ShapeDtypeStruct((tokens, feats), LOW)] * 3,
        input_output_aliases={4 + len(sums) + i: i for i in range(len(earlier))},
        compiler_params=pltpu.CompilerParams(vmem_limit_bytes=32 * 2**20),
        cost_estimate=pl.CostEstimate(
            flops=100 * tokens * tokens * wide, bytes_accessed=16 * tokens * wide, transcendentals=0
        ),
    )(q, k, v, norm, *sums, *earlier)


def context_grad_kernel(offsets, places, *rest):
    w_mine, w_other, a_ref, outs, w_all = rest[:5], rest[5:10], rest[10], rest[11:-1], rest[-1]
    x, y, z, dp = places[0], places[1], places[2], places[3]
    for pieces, half in ((w_mine, dp), (w_other, 1 - dp)):
        own, above, across_a, across_b, below = pieces
        across = jnp.where(pl.program_id(0) == 0, across_a[...], across_b[...])
        for k, piece in enumerate((own[...], above[...], across, below[...])):
            rows = pl.ds(pl.multiple_of((half * 4 + lax.rem(y + k, 4)) * 16, 16), 16)
            w_all[:, rows, :] = piece
    heads, size, width = w_all.shape
    weight = w_all[...].reshape(heads * size, width)
    middle = heads // 2 * size
    for i, k in enumerate(offsets):
        product = dot(a_ref[lax.rem(z + k - x + 4, 4)], weight, ((1,), (1,))).astype(LOW)
        outs[2 * i][...] = product[:, :middle]
        outs[2 * i + 1][...] = product[:, middle:]


def context_grad(offsets, places, w_mine, w_other, layer_grad):
    heads, width = w_mine[0].shape[0], w_mine[0].shape[2]
    group = heads // GROUPS
    half = group // 2 * HEAD_DIM
    piece = pl.BlockSpec((group, 16, width), lambda i, p: (i, 0, 0))
    whole = pl.BlockSpec((group, 16, width), lambda i, p: (0, 0, 0))
    pieces = [piece, piece, whole, whole, piece] * 2
    count = 2 * len(offsets)
    return pl.pallas_call(
        functools.partial(context_grad_kernel, offsets),
        grid_spec=pltpu.PrefetchScalarGridSpec(
            num_scalar_prefetch=1,
            grid=(GROUPS,),
            in_specs=pieces + [pl.BlockSpec(layer_grad.shape, lambda i, p: (0, 0, 0))],
            out_specs=[pl.BlockSpec((PATCHES, half), lambda i, p: (0, i))] * count,
            scratch_shapes=[pltpu.VMEM((group, HEAD_DIM, width), LOW)],
        ),
        out_shape=[jax.ShapeDtypeStruct((PATCHES, GROUPS * half), LOW)] * count,
        compiler_params=pltpu.CompilerParams(vmem_limit_bytes=32 * 2**20),
        cost_estimate=pl.CostEstimate(
            flops=2 * PATCHES * heads * HEAD_DIM, bytes_accessed=2**16, transcendentals=0
        ),
    )(places, *w_mine, *w_other, layer_grad)


def weight_grad_kernel(places, *rest):
    ctx, across_b, a_ref, rest = rest[:4], rest[4], rest[5], rest[6:]
    mine_refs, other_refs, total = rest[:4], rest[4:8], rest[8]
    x, y, z, dp = places[0], places[1], places[2], places[3]
    late = pl.program_id(0) >= pl.num_programs(0) // 2
    acc = None
    for k in range(LAYER):
        block = jnp.where(late, across_b[...], ctx[k][...]) if k == 2 else ctx[k][...]
        term = dot(block, a_ref[lax.rem(z + k - x + 4, 4)], ((1,), (0,)))
        acc = term if acc is None else acc + term
    total[...] = acc
    for h in range(mine_refs[0].shape[0]):
        for slot in range(4):
            part = lax.rem(y + jnp.where(late, SLOTS[1][slot], SLOTS[0][slot]), 4)
            for refs, half in ((mine_refs, dp), (other_refs, 1 - dp)):
                rows = pl.ds(pl.multiple_of(h * HEAD_DIM + (half * 4 + part) * 16, 16), 16)
                refs[slot][h] = total[rows, :].astype(LOW)


def weight_grad(places, contexts, layer_grad):
    feats, tokens = contexts[0].shape
    width = layer_grad.shape[2]
    heads, group = feats // HEAD_DIM, 2
    steps = heads // group
    ctx = pl.BlockSpec((group * HEAD_DIM, tokens), lambda i, p: (i, 0))
    ctx_a = pl.BlockSpec((group * HEAD_DIM, tokens), lambda i, p: (jnp.minimum(i, steps // 2 - 1), 0))
    ctx_b = pl.BlockSpec((group * HEAD_DIM, tokens), lambda i, p: (jnp.maximum(i - steps // 2, 0), 0))
    out = pl.BlockSpec((group, 16, width), lambda i, p: (i, 0, 0))
    return pl.pallas_call(
        weight_grad_kernel,
        grid_spec=pltpu.PrefetchScalarGridSpec(
            num_scalar_prefetch=1,
            grid=(steps,),
            in_specs=[ctx, ctx, ctx_a, ctx, ctx_b]
            + [pl.BlockSpec(layer_grad.shape, lambda i, p: (0, 0, 0))],
            out_specs=[out] * 8,
            scratch_shapes=[pltpu.VMEM((group * HEAD_DIM, width), jnp.float32)],
        ),
        out_shape=[jax.ShapeDtypeStruct((heads, 16, width), LOW)] * 8,
        compiler_params=pltpu.CompilerParams(vmem_limit_bytes=32 * 2**20),
        cost_estimate=pl.CostEstimate(
            flops=2 * PATCHES * feats, bytes_accessed=2**16, transcendentals=0
        ),
    )(places, *contexts, layer_grad)


def shards(grad_out, queries, keys, values, out_weight):
    row_count, feat_width = queries.shape
    head_count = out_weight.shape[0]
    out_width = grad_out.shape[1]
    dp, depth = lax.axis_index("dp"), lax.axis_index("depth")
    y, z_low = depth // 2, lax.rem(depth, 2)
    places = jnp.stack([lax.axis_index("row"), y, lax.axis_index("col"), dp])
    rings = {
        name: [[(i, (i + step) % size) for i in range(size)] for step in steps]
        for name, size, steps in (("row", 4, (1, -1)), ("col", 4, (1, -1)), ("depth", 8, (2, -2)))
    }
    z_pair = [(i, i ^ 1) for i in range(8)]
    core_pair = [(0, 1), (1, 0)]

    def both(axis, for_up, for_down):
        up, down = rings[axis]
        return lax.ppermute(for_up, axis, up), lax.ppermute(for_down, axis, down)

    w_next = lax.ppermute(out_weight, "depth", z_pair)
    g_below, g_above = both("row", grad_out, grad_out)
    context, norm = attention_forward(queries, keys, values)
    c_below, c_above = both("col", context, context)

    w_next = after(w_next, context)
    first = jnp.where(z_low == 0, out_weight, w_next)
    second = jnp.where(z_low == 0, w_next, out_weight)
    w_own = jnp.stack([first, second], axis=1).reshape(head_count, 16, out_width)
    w_own, g_below, g_above = after((w_own, g_below, g_above))
    w_below, w_above = both("depth", w_own, w_own)

    w_below, w_above, c_below, c_above, g_below, g_above = after(
        (w_below, w_above, c_below, c_above, g_below, g_above)
    )
    half = feat_width // 2
    c_across_a, c_across_b = both("col", c_below[:half], c_above[half:])
    half = head_count // 2
    w_across_a, w_across_b = both("depth", w_below[:half], w_above[half:])
    g_across = lax.ppermute(g_below, "row", rings["row"][0])

    w_mine = [w_own, w_above, w_across_a, w_across_b, w_below]
    w_mine, c_across_a, c_across_b, g_across = after((w_mine, c_across_a, c_across_b, g_across))
    layer_grad = jnp.stack([grad_out, g_above, g_across, g_below])
    w_other = [lax.ppermute(piece, "dp", core_pair) for piece in w_mine]
    contexts = (context, c_above, c_across_a, c_below, c_across_b)

    a2, b2 = context_grad((2,), places, w_mine, w_other, layer_grad)
    up_a, down_b = both("col", a2, b2)
    places = after(places, a2, b2)
    a0, b0, a1, b1, a3, b3 = context_grad((0, 1, 3), places, w_mine, w_other, layer_grad)
    b1, a3, up_a, down_b = after((b1, a3, up_a, down_b))
    up_b, down_a = both("col", b1, a3)
    contexts = after(contexts, a0)
    both_halves = weight_grad(places, contexts, layer_grad)
    both_halves = after(both_halves, up_a, down_b)
    paired = [
        add(mine, lax.ppermute(other, "dp", core_pair)).astype(LOW)
        for mine, other in zip(both_halves[:4], both_halves[4:])
    ]
    up, down = both("depth", paired[2], paired[3])
    up, down, up_b, down_a, up_a, down_b = after((up, down, up_b, down_a, up_a, down_b))
    wide = feat_width // GROUPS // 2
    lasts = []
    for g in range(GROUPS):
        cols = slice(g * wide, (g + 1) * wide)
        for_up = add(a1[:, cols], up_a[:, cols]).astype(LOW)
        for_down = add(b3[:, cols], down_b[:, cols]).astype(LOW)
        lasts.append(both("col", for_up, for_down))
    last_up, last_down = both(
        "depth",
        add(paired[1][:half], up[:half]).astype(LOW),
        add(paired[1][half:], down[half:]).astype(LOW),
    )
    summed = jnp.concatenate(
        [
            add(paired[0][:half], down[:half]) + last_up,
            add(paired[0][half:], up[half:]) + last_down,
        ],
        axis=0,
    ).reshape(head_count, 2, 8, out_width)
    mine = jnp.where(z_low == 0, summed[:, 0], summed[:, 1])
    other = jnp.where(z_low == 0, summed[:, 1], summed[:, 0]).astype(LOW)
    other = after(other, lasts[0])
    grad_weight = add(mine, lax.ppermute(other, "depth", z_pair))
    all_tokens = row_count * lax.axis_size("col") * lax.axis_size("dp") * lax.axis_size("depth")
    grad_weight = grad_weight * all_tokens ** (-0.5)

    grads = ()
    for g in range(GROUPS):
        terms = (a0, down_a), (b0, up_b)
        grads = attention_backward(g, queries, keys, values, norm, terms, lasts[g], grads)
    return (*grads, grad_weight)


def solution(mesh):
    in_specs = (
        P(("dp", "depth", "row"), "col"),
        P(("dp", "depth", "col"), "row"),
        P(("dp", "depth", "col"), "row"),
        P(("dp", "depth", "col"), "row"),
        P("row", ("dp", "depth"), "col"),
    )
    out_specs = (
        P(("dp", "depth", "col"), "row"),
        P(("dp", "depth", "col"), "row"),
        P(("dp", "depth", "col"), "row"),
        P("row", ("dp", "depth"), "col"),
    )
    return jax.shard_map(shards, mesh=mesh, in_specs=in_specs, out_specs=out_specs, check_vma=False)
```

```python
import functools

import jax
import jax.numpy as jnp
from jax import lax
from jax.experimental import pallas as pl
from jax.experimental.pallas import tpu as pltpu
from jax.sharding import PartitionSpec as P

HEAD_DIM = 128
PATCHES = 256
SCALE = HEAD_DIM ** (-0.5)
EXP2_SCALE = SCALE * 1.4426950408889634
LAYER = 4
GROUPS = 2
LOW = jnp.bfloat16
SLOTS = ((0, 1, 2, 3), (0, 3, 1, 2))


def dot(a, b, dims):
    return lax.dot_general(a, b, (dims, ((), ())), preferred_element_type=jnp.float32)


def add(a, b):
    return a.astype(jnp.float32) + b.astype(jnp.float32)


def after(value, *earlier):
    return lax.optimization_barrier((value, earlier))[0]


def forward_kernel(q_ref, k_ref, v_ref, ctx_ref, norm_ref):
    for h in range(norm_ref.shape[0]):
        cols = slice(h * HEAD_DIM, (h + 1) * HEAD_DIM)
        scores = dot(k_ref[:, cols], q_ref[:, cols], ((1,), (1,)))
        highest = jnp.max(scores, axis=0, keepdims=True)
        weights = jnp.exp2((scores - highest) * EXP2_SCALE)
        total = jnp.sum(weights, axis=0, keepdims=True)
        probs = (weights * (1.0 / total)).astype(LOW)
        ctx_ref[cols, :] = dot(v_ref[:, cols], probs, ((0,), (0,))).astype(LOW)
        norm_ref[h] = highest * EXP2_SCALE + jnp.log2(total)


def attention_forward(q, k, v):
    tokens, feats = q.shape
    group = 4
    wide = group * HEAD_DIM
    block = pl.BlockSpec((tokens, wide), lambda i: (0, i))
    return pl.pallas_call(
        forward_kernel,
        grid=(feats // wide,),
        in_specs=[block] * 3,
        out_specs=[
            pl.BlockSpec((wide, tokens), lambda i: (i, 0)),
            pl.BlockSpec((group, 1, tokens), lambda i: (i, 0, 0)),
        ],
        out_shape=[
            jax.ShapeDtypeStruct((feats, tokens), LOW),
            jax.ShapeDtypeStruct((feats // HEAD_DIM, 1, tokens), jnp.float32),
        ],
        cost_estimate=pl.CostEstimate(
            flops=4 * tokens * tokens * feats, bytes_accessed=8 * tokens * feats, transcendentals=0
        ),
    )(q, k, v)


def backward_kernel(q_ref, k_ref, v_ref, norm_ref, *rest):
    firsts, seconds = rest[:3], rest[3:6]
    gq_ref, gk_ref, gv_ref = rest[-3:]
    heads = norm_ref.shape[0]
    for h in range(heads):
        cols = slice(h * HEAD_DIM, (h + 1) * HEAD_DIM)
        q, k, v = q_ref[:, cols], k_ref[:, cols], v_ref[:, cols]
        terms, at = (firsts, h) if h < heads // 2 else (seconds, h - heads // 2)
        a, b, c = [ref[:, at * HEAD_DIM : (at + 1) * HEAD_DIM].astype(jnp.float32) for ref in terms]
        g = (a + b + c).astype(LOW)
        scores = dot(k, q, ((1,), (1,)))
        probs = jnp.exp2(scores * EXP2_SCALE - norm_ref[h])
        gv_ref[:, cols] = dot(probs.astype(LOW), g, ((1,), (0,))).astype(LOW)
        grad_probs = dot(v, g, ((1,), (1,)))
        inner = jnp.sum(probs * grad_probs, axis=0, keepdims=True)
        grad_scores = (probs * (grad_probs - inner) * SCALE).astype(LOW)
        gk_ref[:, cols] = dot(grad_scores, q, ((1,), (0,))).astype(LOW)
        gq_ref[:, cols] = dot(grad_scores, k, ((0,), (0,))).astype(LOW)


def attention_backward(q, k, v, norm, terms, last_terms, earlier):
    tokens, feats = q.shape
    wide = feats // GROUPS
    heads = wide // HEAD_DIM
    block = pl.BlockSpec((tokens, wide), lambda i: (0, i))
    half = pl.BlockSpec((tokens, wide // 2), lambda i: (0, i))
    last = pl.BlockSpec((tokens, wide // 2), lambda i: (0, i))
    norms = pl.BlockSpec((heads, 1, tokens), lambda i: (i, 0, 0))
    sums = (*terms[0], last_terms[0], *terms[1], last_terms[1])
    return pl.pallas_call(
        backward_kernel,
        grid=(GROUPS,),
        in_specs=[block] * 3
        + [norms]
        + [half, half, last] * 2
        + [pl.BlockSpec(memory_space=pl.ANY)] * len(earlier),
        out_specs=[block] * 3,
        out_shape=[jax.ShapeDtypeStruct((tokens, feats), LOW)] * 3,
        input_output_aliases={4 + len(sums) + i: i for i in range(len(earlier))},
        compiler_params=pltpu.CompilerParams(vmem_limit_bytes=32 * 2**20),
        cost_estimate=pl.CostEstimate(
            flops=100 * tokens * tokens * wide, bytes_accessed=16 * tokens * wide, transcendentals=0
        ),
    )(q, k, v, norm, *sums, *earlier)


def context_grad_kernel(offsets, places, *rest):
    w_mine, w_other, a_ref, outs, w_all = rest[:5], rest[5:10], rest[10], rest[11:-1], rest[-1]
    x, y, z, dp = places[0], places[1], places[2], places[3]
    for pieces, half in ((w_mine, dp), (w_other, 1 - dp)):
        own, above, across_a, across_b, below = pieces
        across = jnp.where(pl.program_id(0) == 0, across_a[...], across_b[...])
        for k, piece in enumerate((own[...], above[...], across, below[...])):
            rows = pl.ds(pl.multiple_of((half * 4 + lax.rem(y + k, 4)) * 16, 16), 16)
            w_all[:, rows, :] = piece
    heads, size, width = w_all.shape
    weight = w_all[...].reshape(heads * size, width)
    middle = heads // 2 * size
    for i, k in enumerate(offsets):
        product = dot(a_ref[lax.rem(z + k - x + 4, 4)], weight, ((1,), (1,))).astype(LOW)
        outs[2 * i][...] = product[:, :middle]
        outs[2 * i + 1][...] = product[:, middle:]


def context_grad(offsets, places, w_mine, w_other, layer_grad):
    heads, width = w_mine[0].shape[0], w_mine[0].shape[2]
    group = heads // GROUPS
    half = group // 2 * HEAD_DIM
    piece = pl.BlockSpec((group, 16, width), lambda i, p: (i, 0, 0))
    whole = pl.BlockSpec((group, 16, width), lambda i, p: (0, 0, 0))
    pieces = [piece, piece, whole, whole, piece] * 2
    count = 2 * len(offsets)
    return pl.pallas_call(
        functools.partial(context_grad_kernel, offsets),
        grid_spec=pltpu.PrefetchScalarGridSpec(
            num_scalar_prefetch=1,
            grid=(GROUPS,),
            in_specs=pieces + [pl.BlockSpec(layer_grad.shape, lambda i, p: (0, 0, 0))],
            out_specs=[pl.BlockSpec((PATCHES, half), lambda i, p: (0, i))] * count,
            scratch_shapes=[pltpu.VMEM((group, HEAD_DIM, width), LOW)],
        ),
        out_shape=[jax.ShapeDtypeStruct((PATCHES, GROUPS * half), LOW)] * count,
        compiler_params=pltpu.CompilerParams(vmem_limit_bytes=32 * 2**20),
        cost_estimate=pl.CostEstimate(
            flops=2 * PATCHES * heads * HEAD_DIM, bytes_accessed=2**16, transcendentals=0
        ),
    )(places, *w_mine, *w_other, layer_grad)


def weight_grad_kernel(places, *rest):
    ctx, across_b, a_ref, rest = rest[:4], rest[4], rest[5], rest[6:]
    mine_refs, other_refs, total = rest[:4], rest[4:8], rest[8]
    x, y, z, dp = places[0], places[1], places[2], places[3]
    late = pl.program_id(0) >= pl.num_programs(0) // 2
    acc = None
    for k in range(LAYER):
        block = jnp.where(late, across_b[...], ctx[k][...]) if k == 2 else ctx[k][...]
        term = dot(block, a_ref[lax.rem(z + k - x + 4, 4)], ((1,), (0,)))
        acc = term if acc is None else acc + term
    total[...] = acc
    for h in range(mine_refs[0].shape[0]):
        for slot in range(4):
            part = lax.rem(y + jnp.where(late, SLOTS[1][slot], SLOTS[0][slot]), 4)
            for refs, half in ((mine_refs, dp), (other_refs, 1 - dp)):
                rows = pl.ds(pl.multiple_of(h * HEAD_DIM + (half * 4 + part) * 16, 16), 16)
                refs[slot][h] = total[rows, :].astype(LOW)


def weight_grad(places, contexts, layer_grad):
    feats, tokens = contexts[0].shape
    width = layer_grad.shape[2]
    heads, group = feats // HEAD_DIM, 2
    steps = heads // group
    ctx = pl.BlockSpec((group * HEAD_DIM, tokens), lambda i, p: (i, 0))
    ctx_a = pl.BlockSpec((group * HEAD_DIM, tokens), lambda i, p: (jnp.minimum(i, steps // 2 - 1), 0))
    ctx_b = pl.BlockSpec((group * HEAD_DIM, tokens), lambda i, p: (jnp.maximum(i - steps // 2, 0), 0))
    out = pl.BlockSpec((group, 16, width), lambda i, p: (i, 0, 0))
    return pl.pallas_call(
        weight_grad_kernel,
        grid_spec=pltpu.PrefetchScalarGridSpec(
            num_scalar_prefetch=1,
            grid=(steps,),
            in_specs=[ctx, ctx, ctx_a, ctx, ctx_b]
            + [pl.BlockSpec(layer_grad.shape, lambda i, p: (0, 0, 0))],
            out_specs=[out] * 8,
            scratch_shapes=[pltpu.VMEM((group * HEAD_DIM, width), jnp.float32)],
        ),
        out_shape=[jax.ShapeDtypeStruct((heads, 16, width), LOW)] * 8,
        compiler_params=pltpu.CompilerParams(vmem_limit_bytes=32 * 2**20),
        cost_estimate=pl.CostEstimate(
            flops=2 * PATCHES * feats, bytes_accessed=2**16, transcendentals=0
        ),
    )(places, *contexts, layer_grad)


def shards(grad_out, queries, keys, values, out_weight):
    row_count, feat_width = queries.shape
    head_count = out_weight.shape[0]
    out_width = grad_out.shape[1]
    dp, depth = lax.axis_index("dp"), lax.axis_index("depth")
    y, z_low = depth // 2, lax.rem(depth, 2)
    places = jnp.stack([lax.axis_index("row"), y, lax.axis_index("col"), dp])
    rings = {
        name: [[(i, (i + step) % size) for i in range(size)] for step in steps]
        for name, size, steps in (("row", 4, (1, -1)), ("col", 4, (1, -1)), ("depth", 8, (2, -2)))
    }
    z_pair = [(i, i ^ 1) for i in range(8)]
    core_pair = [(0, 1), (1, 0)]

    def both(axis, for_up, for_down):
        up, down = rings[axis]
        return lax.ppermute(for_up, axis, up), lax.ppermute(for_down, axis, down)

    w_next = lax.ppermute(out_weight, "depth", z_pair)
    g_below, g_above = both("row", grad_out, grad_out)
    context, norm = attention_forward(queries, keys, values)
    c_below, c_above = both("col", context, context)

    w_next = after(w_next, context)
    first = jnp.where(z_low == 0, out_weight, w_next)
    second = jnp.where(z_low == 0, w_next, out_weight)
    w_own = jnp.stack([first, second], axis=1).reshape(head_count, 16, out_width)
    w_own, g_below, g_above = after((w_own, g_below, g_above))
    w_below, w_above = both("depth", w_own, w_own)

    w_below, w_above, c_below, c_above, g_below, g_above = after(
        (w_below, w_above, c_below, c_above, g_below, g_above)
    )
    half = feat_width // 2
    c_across_a, c_across_b = both("col", c_below[:half], c_above[half:])
    half = head_count // 2
    w_across_a, w_across_b = both("depth", w_below[:half], w_above[half:])
    g_across = lax.ppermute(g_below, "row", rings["row"][0])

    w_mine = [w_own, w_above, w_across_a, w_across_b, w_below]
    w_mine, c_across_a, c_across_b, g_across = after((w_mine, c_across_a, c_across_b, g_across))
    layer_grad = jnp.stack([grad_out, g_above, g_across, g_below])
    w_other = [lax.ppermute(piece, "dp", core_pair) for piece in w_mine]
    contexts = (context, c_above, c_across_a, c_below, c_across_b)

    a2, b2 = context_grad((2,), places, w_mine, w_other, layer_grad)
    up_a, down_b = both("col", a2, b2)
    places = after(places, a2, b2)
    a0, b0, a1, b1, a3, b3 = context_grad((0, 1, 3), places, w_mine, w_other, layer_grad)
    b1, a3, up_a, down_b = after((b1, a3, up_a, down_b))
    up_b, down_a = both("col", b1, a3)
    contexts = after(contexts, a0)
    both_halves = weight_grad(places, contexts, layer_grad)
    both_halves = after(both_halves, up_a, down_b)
    paired = [
        add(mine, lax.ppermute(other, "dp", core_pair)).astype(LOW)
        for mine, other in zip(both_halves[:4], both_halves[4:])
    ]
    up, down = both("depth", paired[2], paired[3])
    up, down, up_b, down_a, up_a, down_b = after((up, down, up_b, down_a, up_a, down_b))
    for_up = add(a1, up_a).astype(LOW)
    for_down = add(b3, down_b).astype(LOW)
    lasts = [both("col", for_up, for_down)] * GROUPS
    last_up, last_down = both(
        "depth",
        add(paired[1][:half], up[:half]).astype(LOW),
        add(paired[1][half:], down[half:]).astype(LOW),
    )
    last_up, last_down = after((last_up, last_down))
    summed = jnp.concatenate(
        [
            add(paired[0][:half], down[:half]) + last_up,
            add(paired[0][half:], up[half:]) + last_down,
        ],
        axis=0,
    ).reshape(head_count, 2, 8, out_width)
    mine = jnp.where(z_low == 0, summed[:, 0], summed[:, 1])
    other = jnp.where(z_low == 0, summed[:, 1], summed[:, 0]).astype(LOW)
    grad_weight = add(mine, lax.ppermute(other, "depth", z_pair))
    all_tokens = row_count * lax.axis_size("col") * lax.axis_size("dp") * lax.axis_size("depth")
    grad_weight = grad_weight * all_tokens ** (-0.5)

    terms = (a0, down_a), (b0, up_b)
    grads = attention_backward(queries, keys, values, norm, terms, lasts[0], ())
    return (*grads, grad_weight)


def solution(mesh):
    in_specs = (
        P(("dp", "depth", "row"), "col"),
        P(("dp", "depth", "col"), "row"),
        P(("dp", "depth", "col"), "row"),
        P(("dp", "depth", "col"), "row"),
        P("row", ("dp", "depth"), "col"),
    )
    out_specs = (
        P(("dp", "depth", "col"), "row"),
        P(("dp", "depth", "col"), "row"),
        P(("dp", "depth", "col"), "row"),
        P("row", ("dp", "depth"), "col"),
    )
    return jax.shard_map(shards, mesh=mesh, in_specs=in_specs, out_specs=out_specs, check_vma=False)
```
